32 devices in a mesh: subtree: 2 (over x), panel: 4 (over y, core), snap: 4 (over z).
Axes of the slice: x: 2, y: 2, z: 4, core: 2. Of those that a mesh axis runs over, the one named last changes fastest.
Arguments:
- leaf_rhs: bfloat16 [8, 1024, 128], P('subtree', 'panel', 'snap'), may hold values from -6 to 6
- upper_rhs: bfloat16 [7, 1024, 128], P(None, 'panel', 'snap'), may hold values from -6 to 6
- leaf_inv: bfloat16 [8, 1024, 1024], P('subtree', 'panel'), may hold values from -1 to 2, as said below
- upper_inv: bfloat16 [7, 1024, 1024], P(None, 'panel'), may hold values from -1 to 2, as said below
- leaf_panels: bfloat16 [8, 3, 1024, 1024], P('subtree', None, 'panel'), may hold values from -0.09375 to 0.09375
- mid_panels: bfloat16 [4, 2, 1024, 1024], P(None, None, 'panel'), may hold values from -0.09375 to 0.09375
- top_panels: bfloat16 [2, 1024, 1024], P(None, 'panel'), may hold values from -0.09375 to 0.09375
- leaf_widths: int32 [8], P('subtree'), may hold values from 256 to 1024
- upper_widths: int32 [7], replicated, may hold values from 256 to 1024
Outputs:
- leaf_solution: bfloat16 [8, 1024, 128], P('subtree', 'panel', 'snap')
- upper_solution: bfloat16 [7, 1024, 128], P(None, 'panel', 'snap')
The draws below stay inside these ranges and needn't reach their ends.
Inputs may be any that keep to these rules, and one draw needn't show every extreme that they name: `leaf_inv`: each inverse block is a full matrix near the identity. `upper_inv`: each inverse block is a full matrix near the identity.
All inputs are finite; a program needn't handle non-finite values.
Results may differ from the reference program's by a relative error of at most 0.024.
Values may be sent and summed in bfloat16 or wider, within the bound.
A program may use at most 64 MiB of HBM per device.

```python
import math
import jax
import jax.numpy as jnp
from jax import lax

W = 1024
LEAVES = 8
UPPER = 7
SNAPS = 128
N_PANEL = 4


def draw_leaf_inv(key, part):
    noise = jax.random.normal(key, (LEAVES, W, W), jnp.float32)
    return (jnp.eye(W, dtype=jnp.float32)[None] + 0.5 * noise / math.sqrt(W)).astype(jnp.bfloat16)


def draw_upper_inv(key, part):
    noise = jax.random.normal(key, (UPPER, W, W), jnp.float32)
    return (jnp.eye(W, dtype=jnp.float32)[None] + 0.5 * noise / math.sqrt(W)).astype(jnp.bfloat16)


def place_ends(values, stream_key, low, largest):
    dims = values.shape
    index_at = [jax.random.randint(jax.random.fold_in(stream_key, axis), (), 0, dims[axis]) for axis in range(len(dims))]
    values = values.at[tuple(index_at)].set(low)
    longest = dims.index(max(dims))
    index_at[longest] = (index_at[longest] + 1) % dims[longest]
    return values.at[tuple(index_at)].set(largest)


def block_levels(stream_key, extent, split, least, top_value):
    loudness = 1.0
    for position, shards_of in split:
        draws = jax.random.uniform(jax.random.fold_in(jax.random.fold_in(stream_key, 6), position), (shards_of,), jnp.float32, least / len(split), top_value / len(split))
        loudness = loudness * jnp.repeat(jnp.exp(draws), extent[position] // shards_of).reshape((-1,) + (1,) * (len(extent) - 1 - position))
    return loudness


def normal_values(own_key, dims, spread, most, cuts=(), kind=jnp.bfloat16):
    entries = jax.random.normal(own_key, dims, jnp.float32) * spread
    if len(cuts) > 0:
        entries = block_levels(own_key, dims, cuts, -0.22, 0.18) * entries
    return jnp.clip(entries, min=-most, max=most).astype(kind)


def setup_inputs(seed: int = 0) -> dict:
    seeds = jax.random.split(jax.random.key(seed), 10)
    leaf_rhs = normal_values(seeds[0], (LEAVES, W, SNAPS), 1.0, 6.0, ((0, 2), (1, 4), (2, 4)))
    upper_rhs = normal_values(seeds[1], (UPPER, W, SNAPS), 1.0, 6.0, ((1, 4), (2, 4)))
    leaf_inv = draw_leaf_inv(jax.random.fold_in(seeds[9], 71), 0)
    upper_inv = draw_upper_inv(jax.random.fold_in(seeds[9], 71), 0)
    leaf_panels = normal_values(seeds[4], (LEAVES, 3, W, W), (4 * W) ** -0.5, 0.09375, ((0, 2), (2, 4)))
    mid_panels = normal_values(seeds[5], (4, 2, W, W), (4 * W) ** -0.5, 0.09375, ((2, 4),))
    top_panels = normal_values(seeds[6], (2, W, W), (4 * W) ** -0.5, 0.09375, ((1, 4),))
    leaf_widths = place_ends(jax.random.randint(seeds[7], (LEAVES,), W // 4, W + 1), jax.random.fold_in(seeds[7], 1), W // 4, W).astype(jnp.int32)
    upper_widths = place_ends(jax.random.randint(seeds[8], (UPPER,), W // 4, W + 1), jax.random.fold_in(seeds[8], 1), W // 4, W).astype(jnp.int32)
    return dict(leaf_rhs=leaf_rhs, upper_rhs=upper_rhs, leaf_inv=leaf_inv, upper_inv=upper_inv, leaf_panels=leaf_panels, mid_panels=mid_panels, top_panels=top_panels, leaf_widths=leaf_widths, upper_widths=upper_widths)


def live_mask(widths):
    return (jnp.arange(W, dtype=jnp.int32)[None, :] < widths[:, None]).astype(jnp.float32)


def solve_down(inverse, right_side, live_rows):
    masked = (right_side.astype(jnp.float32) * live_rows[:, :, None]).astype(jnp.bfloat16)
    result = jnp.einsum("nij,njc->nic", inverse.astype(jnp.float32), masked.astype(jnp.float32), precision=lax.Precision.HIGHEST)
    return (result * live_rows[:, :, None]).astype(jnp.bfloat16)


def couple(panels, solved):
    return jnp.einsum("nij,njc->nic", panels.astype(jnp.float32), solved.astype(jnp.float32), precision=lax.Precision.HIGHEST)


def blocked(term_pairs):
    running = None
    for matrix, vector in term_pairs:
        count_nodes = matrix.shape[0]
        matrix_blocks = matrix.astype(jnp.float32).reshape(count_nodes, N_PANEL, W // N_PANEL, W)
        vector_blocks = vector.astype(jnp.float32).reshape(count_nodes, N_PANEL, W // N_PANEL, SNAPS)
        block_terms = jnp.einsum("nprw,nprc->npwc", matrix_blocks, vector_blocks, precision=lax.Precision.HIGHEST)
        running = block_terms if running is None else running + block_terms
    rounded = lax.optimization_barrier(running.astype(jnp.bfloat16))
    return jnp.sum(rounded.astype(jnp.float32), axis=1)


def solve_up(inverse, lifted, live_rows):
    masked = (lifted.astype(jnp.float32) * live_rows[:, :, None]).astype(jnp.bfloat16)
    summed = blocked([(inverse, masked)])
    return (summed * live_rows[:, :, None]).astype(jnp.bfloat16)


def reference(leaf_rhs, upper_rhs, leaf_inv, upper_inv, leaf_panels, mid_panels, top_panels, leaf_widths, upper_widths):
    leaf_live = live_mask(leaf_widths)
    upper_live = live_mask(upper_widths)
    leaf_y = solve_down(leaf_inv, leaf_rhs, leaf_live)
    coupled_mid = couple(leaf_panels[:, 0], leaf_y).reshape(4, 2, W, SNAPS).sum(axis=1)
    coupled_high = couple(leaf_panels[:, 1], leaf_y).reshape(2, 4, W, SNAPS).sum(axis=1)
    coupled_root = couple(leaf_panels[:, 2], leaf_y).sum(axis=0, keepdims=True)
    reduced_mid = (upper_rhs[0:4].astype(jnp.float32) - coupled_mid).astype(jnp.bfloat16)
    mid_y = solve_down(upper_inv[0:4], reduced_mid, upper_live[0:4])
    coupled_high = coupled_high + couple(mid_panels[:, 0], mid_y).reshape(2, 2, W, SNAPS).sum(axis=1)
    coupled_root = coupled_root + couple(mid_panels[:, 1], mid_y).sum(axis=0, keepdims=True)
    reduced_high = (upper_rhs[4:6].astype(jnp.float32) - coupled_high).astype(jnp.bfloat16)
    high_y = solve_down(upper_inv[4:6], reduced_high, upper_live[4:6])
    coupled_root = coupled_root + couple(top_panels, high_y).sum(axis=0, keepdims=True)
    reduced_root = (upper_rhs[6:7].astype(jnp.float32) - coupled_root).astype(jnp.bfloat16)
    root_y = solve_down(upper_inv[6:7], reduced_root, upper_live[6:7])

    root_x = solve_up(upper_inv[6:7], root_y, upper_live[6:7])
    carried = blocked([(top_panels, jnp.broadcast_to(root_x, (2, W, SNAPS)))])
    high_x = solve_up(upper_inv[4:6], (high_y.astype(jnp.float32) - carried).astype(jnp.bfloat16), upper_live[4:6])
    carried = blocked([(mid_panels[:, 0], jnp.repeat(high_x, 2, axis=0)), (mid_panels[:, 1], jnp.broadcast_to(root_x, (4, W, SNAPS)))])
    mid_x = solve_up(upper_inv[0:4], (mid_y.astype(jnp.float32) - carried).astype(jnp.bfloat16), upper_live[0:4])
    carried = blocked([(leaf_panels[:, 0], jnp.repeat(mid_x, 2, axis=0)), (leaf_panels[:, 1], jnp.repeat(high_x, 4, axis=0)), (leaf_panels[:, 2], jnp.broadcast_to(root_x, (LEAVES, W, SNAPS)))])
    leaf_x = solve_up(leaf_inv, (leaf_y.astype(jnp.float32) - carried).astype(jnp.bfloat16), leaf_live)
    return leaf_x, jnp.concatenate([mid_x, high_x, root_x], axis=0)
```

```python
import functools

import jax
import jax.numpy as jnp
from jax import lax
from jax.experimental import pallas as pl
from jax.experimental.pallas import tpu as pltpu
from jax.sharding import PartitionSpec as P


def live_mask(widths, full_width):
    return (jnp.arange(full_width, dtype=jnp.int32)[None, :] < widths[:, None]).astype(jnp.float32)


def own_rows(mask_full, own_count):
    return lax.dynamic_slice_in_dim(mask_full, lax.axis_index("panel") * own_count, own_count, 1)


def solve_down(inverse, reduced, mask_full):
    own_count = inverse.shape[1]
    live_cols = mask_full.astype(jnp.bfloat16)
    result = jnp.einsum(
        "nrw,nwc->nrc",
        inverse,
        lax.all_gather(reduced, "panel", axis=1, tiled=True) * live_cols[:, :, None],
        preferred_element_type=jnp.float32,
    )
    return (result * own_rows(mask_full, own_count)[:, :, None]).astype(jnp.bfloat16)


def spread(panels, solved):
    return jnp.einsum(
        "nkrw,nwc->nkrc",
        panels,
        lax.all_gather(solved, "panel", axis=1, tiled=True),
        preferred_element_type=jnp.float32,
    )


def ancestor_tables(global_index, level, count_up):
    offsets = [0, 0, 4, 6]
    slot_ids = jnp.arange(7, dtype=jnp.int32)
    tables = []
    for ancestor_rank in range(count_up):
        target = offsets[level + 1 + ancestor_rank] + jnp.right_shift(
            global_index, 1 + ancestor_rank
        )
        tables.append((slot_ids[None, :] == target[:, None]).astype(jnp.float32))
    return tables


def add_coupled(accum, coupled, tables):
    for ancestor_rank in range(len(tables)):
        accum = accum + jnp.einsum(
            "nrc,nu->urc",
            coupled[:, ancestor_rank],
            tables[ancestor_rank],
            precision=lax.Precision.HIGHEST,
        )
    return accum


def solve_up(inverse, panels, solved, upper_x, tables, mask_full):
    own_count = inverse.shape[1]
    if panels is None:
        reduced = solved
    else:
        picked = jnp.stack(
            [
                jnp.einsum(
                    "nu,urc->nrc",
                    table.astype(jnp.bfloat16),
                    upper_x,
                    preferred_element_type=jnp.float32,
                ).astype(jnp.bfloat16)
                for table in tables
            ],
            axis=1,
        )
        carried = lax.psum_scatter(
            jnp.einsum("nkrw,nkrc->wnc", panels, picked, preferred_element_type=jnp.float32).astype(
                jnp.bfloat16
            ),
            "panel",
            scatter_dimension=0,
            tiled=True,
        ).astype(jnp.float32)
        reduced = (solved.astype(jnp.float32) - jnp.transpose(carried, (1, 0, 2))).astype(
            jnp.bfloat16
        )
    own_live = own_rows(mask_full, own_count)
    masked = reduced * own_live[:, :, None].astype(jnp.bfloat16)
    summed = lax.psum_scatter(
        jnp.einsum("nrw,nrc->wnc", inverse, masked, preferred_element_type=jnp.float32).astype(
            jnp.bfloat16
        ),
        "panel",
        scatter_dimension=0,
        tiled=True,
    ).astype(jnp.float32)
    return (jnp.transpose(summed, (1, 0, 2)) * own_live[:, :, None]).astype(jnp.bfloat16)


def per_device(
    leaf_rhs,
    upper_rhs,
    leaf_inv,
    upper_inv,
    leaf_panels,
    mid_panels,
    top_panels,
    leaf_widths,
    upper_widths,
):
    full_width = leaf_inv.shape[2]
    own_count = leaf_inv.shape[1]
    leaf_count = leaf_inv.shape[0]
    groups = lax.axis_size("subtree")
    group_id = lax.axis_index("subtree")
    leaf_live = live_mask(leaf_widths, full_width)
    upper_live = live_mask(upper_widths, full_width)
    leaf_index = group_id * leaf_count + jnp.arange(leaf_count, dtype=jnp.int32)
    upper_index = jnp.arange(7, dtype=jnp.int32)
    leaf_tables = ancestor_tables(leaf_index, 0, 3)
    mid_tables = ancestor_tables(upper_index[0:4], 1, 2)
    high_tables = ancestor_tables(upper_index[4:6] - 4, 2, 1)
    top_stack = top_panels[:, None]
    leaf_sol = solve_down(leaf_inv, leaf_rhs, leaf_live)
    coupled_sum = jnp.zeros((7, own_count, leaf_rhs.shape[2]), jnp.float32)
    coupled_sum = add_coupled(coupled_sum, spread(leaf_panels, leaf_sol), leaf_tables)
    column_share = leaf_rhs.shape[2] // groups
    coupled_sum = lax.psum_scatter(
        coupled_sum.astype(jnp.bfloat16), "subtree", scatter_dimension=2, tiled=True
    ).astype(jnp.float32)
    upper_part = lax.dynamic_slice_in_dim(upper_rhs, group_id * column_share, column_share, 2)
    mid_sol = solve_down(
        upper_inv[0:4],
        (upper_part[0:4].astype(jnp.float32) - coupled_sum[0:4]).astype(jnp.bfloat16),
        upper_live[0:4],
    )
    coupled_sum = add_coupled(coupled_sum, spread(mid_panels, mid_sol), mid_tables)
    high_sol = solve_down(
        upper_inv[4:6],
        (upper_part[4:6].astype(jnp.float32) - coupled_sum[4:6]).astype(jnp.bfloat16),
        upper_live[4:6],
    )
    coupled_sum = add_coupled(coupled_sum, spread(top_stack, high_sol), high_tables)
    root_sol = solve_down(
        upper_inv[6:7],
        (upper_part[6:7].astype(jnp.float32) - coupled_sum[6:7]).astype(jnp.bfloat16),
        upper_live[6:7],
    )
    column_count = upper_part.shape[2]
    zero_mid = jnp.zeros((4, own_count, column_count), jnp.bfloat16)
    zero_high = jnp.zeros((2, own_count, column_count), jnp.bfloat16)
    root_x = solve_up(upper_inv[6:7], None, root_sol, None, None, upper_live[6:7])
    upper_x = jnp.concatenate([zero_mid, zero_high, root_x], axis=0)
    high_x = solve_up(upper_inv[4:6], top_stack, high_sol, upper_x, high_tables, upper_live[4:6])
    upper_x = jnp.concatenate([zero_mid, high_x, root_x], axis=0)
    mid_x = solve_up(upper_inv[0:4], mid_panels, mid_sol, upper_x, mid_tables, upper_live[0:4])
    upper_x = jnp.concatenate([mid_x, high_x, root_x], axis=0)
    upper_x = lax.all_gather(upper_x, "subtree", axis=2, tiled=True)
    leaf_x = solve_up(leaf_inv, leaf_panels, leaf_sol, upper_x, leaf_tables, leaf_live)
    return (leaf_x, upper_x)


def nt(left, right):
    return lax.dot_general(
        left, right, (((1,), (1,)), ((), ())), preferred_element_type=jnp.float32
    )


def nn(left, right):
    return jnp.dot(left, right, preferred_element_type=jnp.float32)


def tree_kernel(
    n,
    leaf_widths,
    upper_widths,
    leaf_rhs,
    upper_rhs,
    leaf_inv_h,
    upper_inv_h,
    leaf_panels_h,
    mid_panels_h,
    top_panels_h,
    leaf_out,
    upper_out,
    leaf_inv,
    upper_inv,
    leaf_panels,
    mid_panels,
    top_panel,
    r_full,
    y_full,
    root_full,
    part_c,
    part_s,
    recv_c,
    recv_s,
    accum,
    mine,
    theirs,
    load_sem,
    send_sem,
    recv_sem,
    cross_send,
    cross_recv,
):
    g = lax.axis_index("subtree")
    p = lax.axis_index("panel")
    rows = leaf_inv.shape[1]
    far = n // 2
    chip, core = p // 2, p % 2
    steps = list(range(2, n)) + [1]

    def ahead(k):
        return ((chip + k // 2) % far) * 2 + (core + k % 2) % 2

    def behind(k):
        return ((chip + far - k // 2) % far) * 2 + (core + k % 2) % 2

    def cols(index):
        return pl.ds(pl.multiple_of(index * rows, rows), rows)

    own = cols(p)

    barrier = pltpu.get_barrier_semaphore()
    for k in range(1, n):
        pl.semaphore_signal(barrier, inc=1, device_id={"panel": ahead(k)})
    for k in range(n):
        pl.semaphore_signal(barrier, inc=1, device_id={"subtree": 1 - g, "panel": ahead(k)})

    loads = {}

    def load(key, src, dst):
        loads[key] = pltpu.make_async_copy(src, dst, load_sem.at[len(loads)])
        loads[key].start()

    for s in range(4):
        load(("inv", s), leaf_inv_h.at[s], leaf_inv.at[s])
    for s in range(4):
        load(("pan", s), leaf_panels_h.at[s], leaf_panels.at[s])
    for i in range(2):
        load(("inv", 4 + i), upper_inv_h.at[2 * g + i], upper_inv.at[i])
    for i in range(2):
        load(("pan", 4 + i), mid_panels_h.at[2 * g + i], mid_panels.at[i])
    load(("inv", 6), upper_inv_h.at[4 + g], upper_inv.at[2])
    load(("pan", 6), top_panels_h.at[g], top_panel)
    load(("inv", 7), upper_inv_h.at[6], upper_inv.at[3])

    def inverse(s):
        return leaf_inv[s] if s < 4 else upper_inv[s - 4]

    upper_index = {4: 2 * g, 5: 2 * g + 1, 6: 4 + g, 7: 6}
    row_id = lax.broadcasted_iota(jnp.int32, (1, rows), 1) + p * rows

    def masked(s, value):
        width = leaf_widths[s] if s < 4 else upper_widths[upper_index[s]]
        return jnp.where(row_id < width, value, 0.0)

    pending = []

    def send(src, dst, ssem, rsem, device):
        copy = pltpu.make_async_remote_copy(
            src_ref=src, dst_ref=dst, send_sem=ssem, recv_sem=rsem, device_id=device
        )
        copy.start()
        pending.append(copy)

    def arrived(dst, ssem, rsem):
        pltpu.make_async_remote_copy(
            src_ref=dst, dst_ref=dst, send_sem=ssem, recv_sem=rsem, device_id={"panel": ahead(1)}
        ).wait_recv()

    def gather_start(e, full, s, value):
        full[s, :, own] = value
        for k in steps:
            block = full.at[s, :, own]
            send(block, block, send_sem.at[e, s, k - 1], recv_sem.at[e, s, k - 1], {"panel": ahead(k)})

    def gather_wait(e, full, s):
        for k in reversed(steps):
            arrived(full.at[s, :, cols(behind(k))], send_sem.at[e, s, k - 1], recv_sem.at[e, s, k - 1])
        return full[s]

    def scatter_start(e, part, recv, s, value):
        part[s] = value.astype(jnp.bfloat16)
        for k in steps:
            send(
                part.at[s, :, cols(ahead(k))],
                recv.at[s, k - 1],
                send_sem.at[e, s, k - 1],
                recv_sem.at[e, s, k - 1],
                {"panel": ahead(k)},
            )

    def scatter_wait(e, part, recv, s):
        total = part[s, :, own].astype(jnp.float32)
        for k in reversed(steps):
            arrived(recv.at[s, k - 1], send_sem.at[e, s, k - 1], recv_sem.at[e, s, k - 1])
            total = total + recv[s, k - 1].astype(jnp.float32)
        return total

    rhs_masked = [masked(s, leaf_rhs[s].astype(jnp.float32)).astype(jnp.bfloat16) for s in range(4)]
    pl.semaphore_wait(barrier, 2 * n - 1)
    for s in range(4):
        gather_start(0, r_full, s, rhs_masked[s])

    def solve_y(s):
        full = gather_wait(0, r_full, s)
        loads[("inv", s)].wait()
        result = masked(s, nt(full, inverse(s))).astype(jnp.bfloat16)
        gather_start(1, y_full, s, result)

    def reduce_rhs(s, coupled):
        value = (upper_rhs[upper_index[s]].astype(jnp.float32) - coupled).astype(jnp.bfloat16)
        gather_start(0, r_full, s, masked(s, value.astype(jnp.float32)).astype(jnp.bfloat16))

    for s in range(4):
        solve_y(s)
    to_mid = []
    for s in range(4):
        full = gather_wait(1, y_full, s)
        loads[("pan", s)].wait()
        to_mid.append(nt(full, leaf_panels[s, 0]))
        if s % 2 == 1:
            reduce_rhs(4 + s // 2, to_mid[s - 1] + to_mid[s])
    to_high = nt(y_full[0], leaf_panels[0, 1])
    for s in range(1, 4):
        to_high = to_high + nt(y_full[s], leaf_panels[s, 1])
    solve_y(4)
    solve_y(5)
    to_root = nt(y_full[0], leaf_panels[0, 2])
    for s in range(1, 4):
        to_root = to_root + nt(y_full[s], leaf_panels[s, 2])
    for s in (4, 5):
        full = gather_wait(1, y_full, s)
        loads[("pan", s)].wait()
        to_high = to_high + nt(full, mid_panels[s - 4, 0])
    reduce_rhs(6, to_high)
    for s in (4, 5):
        to_root = to_root + nt(y_full[s], mid_panels[s - 4, 1])
    solve_y(6)
    full = gather_wait(1, y_full, 6)
    loads[("pan", 6)].wait()
    to_root = to_root + nt(full, top_panel[...])

    base = jnp.where(g == 0, upper_rhs[6].astype(jnp.float32), 0.0)
    root_full[g, :, own] = masked(7, base - to_root).astype(jnp.bfloat16)
    block = root_full.at[g, :, own]
    for k in steps + [0]:
        send(
            block,
            block,
            cross_send.at[k],
            cross_recv.at[k],
            {"subtree": 1 - g, "panel": ahead(k)},
        )
        if k > 0:
            send(block, block, send_sem.at[0, 7, k - 1], recv_sem.at[0, 7, k - 1], {"panel": ahead(k)})
    loads[("inv", 7)].wait()
    for k in reversed(steps):
        arrived(
            root_full.at[g, :, cols(behind(k))], send_sem.at[0, 7, k - 1], recv_sem.at[0, 7, k - 1]
        )
    for k in [0] + steps:
        arrived(root_full.at[1 - g, :, cols(behind(k))], cross_send.at[k], cross_recv.at[k])
    reduced = (root_full[0].astype(jnp.float32) + root_full[1].astype(jnp.float32)).astype(jnp.bfloat16)
    lifted = masked(7, nt(reduced, inverse(7))).astype(jnp.bfloat16)

    def lift(s):
        own_y = y_full[s, :, own].astype(jnp.float32)
        value = (own_y - scatter_wait(2, part_c, recv_c, s)).astype(jnp.bfloat16)
        value = masked(s, value.astype(jnp.float32)).astype(jnp.bfloat16)
        scatter_start(3, part_s, recv_s, s, nn(value, inverse(s)))

    def solved(s):
        return masked(s, scatter_wait(3, part_s, recv_s, s)).astype(jnp.bfloat16)

    scatter_start(3, part_s, recv_s, 7, nn(lifted, inverse(7)))
    root_x = solved(7)
    scatter_start(2, part_c, recv_c, 6, nn(root_x, top_panel[...]))
    upper_out[6] = root_x
    for i in range(2):
        accum[4 + i] = nn(root_x, mid_panels[i, 1])
    lift(6)
    for s in range(4):
        accum[s] = nn(root_x, leaf_panels[s, 2])
    high_x = solved(6)
    for s in (4, 5):
        scatter_start(2, part_c, recv_c, s, accum[s] + nn(high_x, mid_panels[s - 4, 0]))

    def share(i, s, value):
        upper_out[upper_index[s]] = value
        mine[i] = value
        send(mine.at[i], theirs.at[i], cross_send.at[n + i], cross_recv.at[n + i], {"subtree": 1 - g})

    share(2, 6, high_x)
    for s in range(4):
        accum[s] = accum[s] + nn(high_x, leaf_panels[s, 1])
    lift(4)
    lift(5)
    for i in range(2):
        mid_x = solved(4 + i)
        for s in (2 * i, 2 * i + 1):
            scatter_start(2, part_c, recv_c, s, accum[s] + nn(mid_x, leaf_panels[s, 0]))
        share(i, 4 + i, mid_x)
    for s in range(4):
        lift(s)
    for i, slot in ((0, 2 * (1 - g)), (1, 2 * (1 - g) + 1), (2, 5 - g)):
        arrived(theirs.at[i], cross_send.at[n + i], cross_recv.at[n + i])
        upper_out[slot] = theirs[i]
    for s in range(4):
        leaf_out[s] = solved(s)
    for copy in pending:
        copy.wait_send()


def half_tree(
    n,
    leaf_rhs,
    upper_rhs,
    leaf_inv,
    upper_inv,
    leaf_panels,
    mid_panels,
    top_panels,
    leaf_widths,
    upper_widths,
):
    rows, width, count = leaf_inv.shape[1], leaf_inv.shape[2], leaf_rhs.shape[2]
    low = jnp.bfloat16
    smem = pl.BlockSpec(memory_space=pltpu.SMEM)
    vmem = pl.BlockSpec(memory_space=pltpu.VMEM)
    hbm = pl.BlockSpec(memory_space=pltpu.HBM)
    leaf_t, upper_t = pl.pallas_call(
        functools.partial(tree_kernel, n),
        out_shape=[
            jax.ShapeDtypeStruct((4, count, rows), low),
            jax.ShapeDtypeStruct((7, count, rows), low),
        ],
        in_specs=[smem, smem, vmem, vmem, hbm, hbm, hbm, hbm, hbm],
        out_specs=[vmem, vmem],
        scratch_shapes=[
            pltpu.VMEM((4, rows, width), low),
            pltpu.VMEM((4, rows, width), low),
            pltpu.VMEM((4, 3, rows, width), low),
            pltpu.VMEM((2, 2, rows, width), low),
            pltpu.VMEM((rows, width), low),
            pltpu.VMEM((7, count, width), low),
            pltpu.VMEM((7, count, width), low),
            pltpu.VMEM((2, count, width), low),
            pltpu.VMEM((7, count, width), low),
            pltpu.VMEM((8, count, width), low),
            pltpu.VMEM((7, n - 1, count, rows), low),
            pltpu.VMEM((8, n - 1, count, rows), low),
            pltpu.VMEM((6, count, width), jnp.float32),
            pltpu.VMEM((3, count, rows), low),
            pltpu.VMEM((3, count, rows), low),
            pltpu.SemaphoreType.DMA((15,)),
            pltpu.SemaphoreType.DMA((4, 8, n - 1)),
            pltpu.SemaphoreType.DMA((4, 8, n - 1)),
            pltpu.SemaphoreType.DMA((n + 3,)),
            pltpu.SemaphoreType.DMA((n + 3,)),
        ],
        compiler_params=pltpu.CompilerParams(
            collective_id=0, has_side_effects=True, vmem_limit_bytes=48 * 1024 * 1024
        ),
    )(
        leaf_widths,
        upper_widths,
        jnp.swapaxes(leaf_rhs, 1, 2),
        jnp.swapaxes(upper_rhs, 1, 2),
        leaf_inv,
        upper_inv,
        leaf_panels,
        mid_panels,
        top_panels,
    )
    return jnp.swapaxes(leaf_t, 1, 2), jnp.swapaxes(upper_t, 1, 2)


def solution(mesh):
    in_specs = (
        P("subtree", "panel", "snap"),
        P(None, "panel", "snap"),
        P("subtree", "panel", None),
        P(None, "panel", None),
        P("subtree", None, "panel", None),
        P(None, None, "panel", None),
        P(None, "panel", None),
        P("subtree"),
        P(),
    )
    out_specs = (P("subtree", "panel", "snap"), P(None, "panel", "snap"))
    panel_count = mesh.shape["panel"]
    if mesh.shape["subtree"] == 2 and panel_count % 2 == 0:
        body = functools.partial(half_tree, panel_count)
    else:
        body = per_device
    return jax.shard_map(
        body, mesh=mesh, in_specs=in_specs, out_specs=out_specs, check_vma=False
    )
```

```python
import functools

import jax
import jax.numpy as jnp
from jax import lax
from jax.experimental import pallas as pl
from jax.experimental.pallas import tpu as pltpu
from jax.sharding import PartitionSpec as P


def live_mask(widths, full_width):
    return (jnp.arange(full_width, dtype=jnp.int32)[None, :] < widths[:, None]).astype(jnp.float32)


def own_rows(mask_full, own_count):
    return lax.dynamic_slice_in_dim(mask_full, lax.axis_index("panel") * own_count, own_count, 1)


def solve_down(inverse, reduced, mask_full):
    own_count = inverse.shape[1]
    live_cols = mask_full.astype(jnp.bfloat16)
    result = jnp.einsum(
        "nrw,nwc->nrc",
        inverse,
        lax.all_gather(reduced, "panel", axis=1, tiled=True) * live_cols[:, :, None],
        preferred_element_type=jnp.float32,
    )
    return (result * own_rows(mask_full, own_count)[:, :, None]).astype(jnp.bfloat16)


def spread(panels, solved):
    return jnp.einsum(
        "nkrw,nwc->nkrc",
        panels,
        lax.all_gather(solved, "panel", axis=1, tiled=True),
        preferred_element_type=jnp.float32,
    )


def ancestor_tables(global_index, level, count_up):
    offsets = [0, 0, 4, 6]
    slot_ids = jnp.arange(7, dtype=jnp.int32)
    tables = []
    for ancestor_rank in range(count_up):
        target = offsets[level + 1 + ancestor_rank] + jnp.right_shift(
            global_index, 1 + ancestor_rank
        )
        tables.append((slot_ids[None, :] == target[:, None]).astype(jnp.float32))
    return tables


def add_coupled(accum, coupled, tables):
    for ancestor_rank in range(len(tables)):
        accum = accum + jnp.einsum(
            "nrc,nu->urc",
            coupled[:, ancestor_rank],
            tables[ancestor_rank],
            precision=lax.Precision.HIGHEST,
        )
    return accum


def solve_up(inverse, panels, solved, upper_x, tables, mask_full):
    own_count = inverse.shape[1]
    if panels is None:
        reduced = solved
    else:
        picked = jnp.stack(
            [
                jnp.einsum(
                    "nu,urc->nrc",
                    table.astype(jnp.bfloat16),
                    upper_x,
                    preferred_element_type=jnp.float32,
                ).astype(jnp.bfloat16)
                for table in tables
            ],
            axis=1,
        )
        carried = lax.psum_scatter(
            jnp.einsum("nkrw,nkrc->wnc", panels, picked, preferred_element_type=jnp.float32).astype(
                jnp.bfloat16
            ),
            "panel",
            scatter_dimension=0,
            tiled=True,
        ).astype(jnp.float32)
        reduced = (solved.astype(jnp.float32) - jnp.transpose(carried, (1, 0, 2))).astype(
            jnp.bfloat16
        )
    own_live = own_rows(mask_full, own_count)
    masked = reduced * own_live[:, :, None].astype(jnp.bfloat16)
    summed = lax.psum_scatter(
        jnp.einsum("nrw,nrc->wnc", inverse, masked, preferred_element_type=jnp.float32).astype(
            jnp.bfloat16
        ),
        "panel",
        scatter_dimension=0,
        tiled=True,
    ).astype(jnp.float32)
    return (jnp.transpose(summed, (1, 0, 2)) * own_live[:, :, None]).astype(jnp.bfloat16)


def per_device(
    leaf_rhs,
    upper_rhs,
    leaf_inv,
    upper_inv,
    leaf_panels,
    mid_panels,
    top_panels,
    leaf_widths,
    upper_widths,
):
    full_width = leaf_inv.shape[2]
    own_count = leaf_inv.shape[1]
    leaf_count = leaf_inv.shape[0]
    groups = lax.axis_size("subtree")
    group_id = lax.axis_index("subtree")
    leaf_live = live_mask(leaf_widths, full_width)
    upper_live = live_mask(upper_widths, full_width)
    leaf_index = group_id * leaf_count + jnp.arange(leaf_count, dtype=jnp.int32)
    upper_index = jnp.arange(7, dtype=jnp.int32)
    leaf_tables = ancestor_tables(leaf_index, 0, 3)
    mid_tables = ancestor_tables(upper_index[0:4], 1, 2)
    high_tables = ancestor_tables(upper_index[4:6] - 4, 2, 1)
    top_stack = top_panels[:, None]
    leaf_sol = solve_down(leaf_inv, leaf_rhs, leaf_live)
    coupled_sum = jnp.zeros((7, own_count, leaf_rhs.shape[2]), jnp.float32)
    coupled_sum = add_coupled(coupled_sum, spread(leaf_panels, leaf_sol), leaf_tables)
    column_share = leaf_rhs.shape[2] // groups
    coupled_sum = lax.psum_scatter(
        coupled_sum.astype(jnp.bfloat16), "subtree", scatter_dimension=2, tiled=True
    ).astype(jnp.float32)
    upper_part = lax.dynamic_slice_in_dim(upper_rhs, group_id * column_share, column_share, 2)
    mid_sol = solve_down(
        upper_inv[0:4],
        (upper_part[0:4].astype(jnp.float32) - coupled_sum[0:4]).astype(jnp.bfloat16),
        upper_live[0:4],
    )
    coupled_sum = add_coupled(coupled_sum, spread(mid_panels, mid_sol), mid_tables)
    high_sol = solve_down(
        upper_inv[4:6],
        (upper_part[4:6].astype(jnp.float32) - coupled_sum[4:6]).astype(jnp.bfloat16),
        upper_live[4:6],
    )
    coupled_sum = add_coupled(coupled_sum, spread(top_stack, high_sol), high_tables)
    root_sol = solve_down(
        upper_inv[6:7],
        (upper_part[6:7].astype(jnp.float32) - coupled_sum[6:7]).astype(jnp.bfloat16),
        upper_live[6:7],
    )
    column_count = upper_part.shape[2]
    zero_mid = jnp.zeros((4, own_count, column_count), jnp.bfloat16)
    zero_high = jnp.zeros((2, own_count, column_count), jnp.bfloat16)
    root_x = solve_up(upper_inv[6:7], None, root_sol, None, None, upper_live[6:7])
    upper_x = jnp.concatenate([zero_mid, zero_high, root_x], axis=0)
    high_x = solve_up(upper_inv[4:6], top_stack, high_sol, upper_x, high_tables, upper_live[4:6])
    upper_x = jnp.concatenate([zero_mid, high_x, root_x], axis=0)
    mid_x = solve_up(upper_inv[0:4], mid_panels, mid_sol, upper_x, mid_tables, upper_live[0:4])
    upper_x = jnp.concatenate([mid_x, high_x, root_x], axis=0)
    upper_x = lax.all_gather(upper_x, "subtree", axis=2, tiled=True)
    leaf_x = solve_up(leaf_inv, leaf_panels, leaf_sol, upper_x, leaf_tables, leaf_live)
    return (leaf_x, upper_x)


def nt(left, right):
    return lax.dot_general(
        left, right, (((1,), (1,)), ((), ())), preferred_element_type=jnp.float32
    )


def nn(left, right):
    return jnp.dot(left, right, preferred_element_type=jnp.float32)


def tree_kernel(
    n,
    leaf_widths_h,
    upper_widths_h,
    leaf_rhs_h,
    upper_rhs_h,
    leaf_inv_h,
    upper_inv_h,
    leaf_panels_h,
    mid_panels_h,
    top_panels_h,
    leaf_out_h,
    upper_out_h,
    leaf_widths,
    upper_widths,
    leaf_rhs,
    upper_rhs,
    leaf_inv,
    upper_inv,
    leaf_panels,
    mid_panels,
    top_panel,
    r_full,
    y_full,
    root_full,
    part_c,
    part_s,
    recv_c,
    recv_s,
    accum,
    mine,
    theirs,
    leaf_out,
    root_out,
    load_sem,
    send_sem,
    recv_sem,
    cross_send,
    cross_recv,
    store_sem,
):
    g = lax.axis_index("subtree")
    p = lax.axis_index("panel")
    rows = leaf_inv.shape[1]
    far = n // 2
    chip, core = p // 2, p % 2
    steps = list(range(2, n)) + [1]

    def ahead(k):
        return ((chip + k // 2) % far) * 2 + (core + k % 2) % 2

    def behind(k):
        return ((chip + far - k // 2) % far) * 2 + (core + k % 2) % 2

    def cols(index):
        return pl.ds(pl.multiple_of(index * rows, rows), rows)

    own = cols(p)

    barrier = pltpu.get_barrier_semaphore()
    for k in range(1, n):
        pl.semaphore_signal(barrier, inc=1, device_id={"panel": ahead(k)})
    for k in range(n):
        pl.semaphore_signal(barrier, inc=1, device_id={"subtree": 1 - g, "panel": ahead(k)})

    stores = []

    def store(src, dst):
        stores.append(pltpu.make_async_copy(src, dst, store_sem.at[len(stores)]))
        stores[-1].start()

    loads = {}

    def load(key, src, dst):
        loads[key] = pltpu.make_async_copy(src, dst, load_sem.at[len(loads)])
        loads[key].start()

    load("leaf_rhs", leaf_rhs_h, leaf_rhs)
    load("leaf_widths", leaf_widths_h, leaf_widths)
    load("upper_widths", upper_widths_h, upper_widths)
    for s in range(4):
        load(("inv", s), leaf_inv_h.at[s], leaf_inv.at[s])
    load("upper_rhs", upper_rhs_h, upper_rhs)
    for s in range(4):
        load(("pan", s), leaf_panels_h.at[s], leaf_panels.at[s])
    for i in range(2):
        load(("inv", 4 + i), upper_inv_h.at[2 * g + i], upper_inv.at[i])
    for i in range(2):
        load(("pan", 4 + i), mid_panels_h.at[2 * g + i], mid_panels.at[i])
    load(("inv", 6), upper_inv_h.at[4 + g], upper_inv.at[2])
    load(("pan", 6), top_panels_h.at[g], top_panel)
    load(("inv", 7), upper_inv_h.at[6], upper_inv.at[3])

    def inverse(s):
        return leaf_inv[s] if s < 4 else upper_inv[s - 4]

    upper_index = {4: 2 * g, 5: 2 * g + 1, 6: 4 + g, 7: 6}
    row_id = lax.broadcasted_iota(jnp.int32, (1, rows), 1) + p * rows

    def masked(s, value):
        width = leaf_widths[s] if s < 4 else upper_widths[upper_index[s]]
        return jnp.where(row_id < width, value, 0.0)

    pending = []

    def send(src, dst, ssem, rsem, device):
        copy = pltpu.make_async_remote_copy(
            src_ref=src, dst_ref=dst, send_sem=ssem, recv_sem=rsem, device_id=device
        )
        copy.start()
        pending.append(copy)

    def arrived(dst, ssem, rsem):
        pltpu.make_async_remote_copy(
            src_ref=dst, dst_ref=dst, send_sem=ssem, recv_sem=rsem, device_id={"panel": ahead(1)}
        ).wait_recv()

    def gather_start(e, full, s, value):
        full[s, :, own] = value
        for k in steps:
            block = full.at[s, :, own]
            send(block, block, send_sem.at[e, s, k - 1], recv_sem.at[e, s, k - 1], {"panel": ahead(k)})

    def gather_wait(e, full, s):
        for k in reversed(steps):
            arrived(full.at[s, :, cols(behind(k))], send_sem.at[e, s, k - 1], recv_sem.at[e, s, k - 1])
        return full[s]

    def scatter_start(e, part, recv, s, value):
        part[s] = value.astype(jnp.bfloat16)
        for k in steps:
            send(
                part.at[s, :, cols(ahead(k))],
                recv.at[s, k - 1],
                send_sem.at[e, s, k - 1],
                recv_sem.at[e, s, k - 1],
                {"panel": ahead(k)},
            )

    def scatter_wait(e, part, recv, s):
        total = part[s, :, own].astype(jnp.float32)
        for k in reversed(steps):
            arrived(recv.at[s, k - 1], send_sem.at[e, s, k - 1], recv_sem.at[e, s, k - 1])
            total = total + recv[s, k - 1].astype(jnp.float32)
        return total

    for key in ("leaf_rhs", "leaf_widths", "upper_widths"):
        loads[key].wait()
    rhs_masked = [masked(s, leaf_rhs[s].astype(jnp.float32)).astype(jnp.bfloat16) for s in range(4)]
    pl.semaphore_wait(barrier, 2 * n - 1)
    for s in range(4):
        gather_start(0, r_full, s, rhs_masked[s])

    def solve_y(s):
        full = gather_wait(0, r_full, s)
        loads[("inv", s)].wait()
        result = masked(s, nt(full, inverse(s))).astype(jnp.bfloat16)
        gather_start(1, y_full, s, result)

    def reduce_rhs(s, coupled):
        value = (upper_rhs[upper_index[s]].astype(jnp.float32) - coupled).astype(jnp.bfloat16)
        gather_start(0, r_full, s, masked(s, value.astype(jnp.float32)).astype(jnp.bfloat16))

    for s in range(4):
        solve_y(s)
    loads["upper_rhs"].wait()
    to_mid = []
    for s in range(4):
        full = gather_wait(1, y_full, s)
        loads[("pan", s)].wait()
        to_mid.append(nt(full, leaf_panels[s, 0]))
        if s % 2 == 1:
            reduce_rhs(4 + s // 2, to_mid[s - 1] + to_mid[s])
    to_high = nt(y_full[0], leaf_panels[0, 1])
    for s in range(1, 4):
        to_high = to_high + nt(y_full[s], leaf_panels[s, 1])
    solve_y(4)
    solve_y(5)
    to_root = nt(y_full[0], leaf_panels[0, 2])
    for s in range(1, 4):
        to_root = to_root + nt(y_full[s], leaf_panels[s, 2])
    for s in (4, 5):
        full = gather_wait(1, y_full, s)
        loads[("pan", s)].wait()
        to_high = to_high + nt(full, mid_panels[s - 4, 0])
    reduce_rhs(6, to_high)
    for s in (4, 5):
        to_root = to_root + nt(y_full[s], mid_panels[s - 4, 1])
    solve_y(6)
    full = gather_wait(1, y_full, 6)
    loads[("pan", 6)].wait()
    to_root = to_root + nt(full, top_panel[...])

    base = jnp.where(g == 0, upper_rhs[6].astype(jnp.float32), 0.0)
    root_full[g, :, own] = masked(7, base - to_root).astype(jnp.bfloat16)
    block = root_full.at[g, :, own]
    for k in steps + [0]:
        send(
            block,
            block,
            cross_send.at[k],
            cross_recv.at[k],
            {"subtree": 1 - g, "panel": ahead(k)},
        )
        if k > 0:
            send(block, block, send_sem.at[0, 7, k - 1], recv_sem.at[0, 7, k - 1], {"panel": ahead(k)})
    loads[("inv", 7)].wait()
    for k in reversed(steps):
        arrived(
            root_full.at[g, :, cols(behind(k))], send_sem.at[0, 7, k - 1], recv_sem.at[0, 7, k - 1]
        )
    for k in [0] + steps:
        arrived(root_full.at[1 - g, :, cols(behind(k))], cross_send.at[k], cross_recv.at[k])
    reduced = (root_full[0].astype(jnp.float32) + root_full[1].astype(jnp.float32)).astype(jnp.bfloat16)
    lifted = masked(7, nt(reduced, inverse(7))).astype(jnp.bfloat16)

    def lift(s):
        own_y = y_full[s, :, own].astype(jnp.float32)
        value = (own_y - scatter_wait(2, part_c, recv_c, s)).astype(jnp.bfloat16)
        value = masked(s, value.astype(jnp.float32)).astype(jnp.bfloat16)
        scatter_start(3, part_s, recv_s, s, nn(value, inverse(s)))

    def solved(s):
        return masked(s, scatter_wait(3, part_s, recv_s, s)).astype(jnp.bfloat16)

    scatter_start(3, part_s, recv_s, 7, nn(lifted, inverse(7)))
    root_x = solved(7)
    scatter_start(2, part_c, recv_c, 6, nn(root_x, top_panel[...]))
    root_out[...] = root_x
    store(root_out, upper_out_h.at[6])
    for i in range(2):
        accum[4 + i] = nn(root_x, mid_panels[i, 1])
    lift(6)
    for s in range(4):
        accum[s] = nn(root_x, leaf_panels[s, 2])
    high_x = solved(6)
    for s in (4, 5):
        scatter_start(2, part_c, recv_c, s, accum[s] + nn(high_x, mid_panels[s - 4, 0]))

    def share(i, s, value):
        mine[i] = value
        store(mine.at[i], upper_out_h.at[upper_index[s]])
        send(mine.at[i], theirs.at[i], cross_send.at[n + i], cross_recv.at[n + i], {"subtree": 1 - g})

    share(2, 6, high_x)
    for s in range(4):
        accum[s] = accum[s] + nn(high_x, leaf_panels[s, 1])
    lift(4)
    lift(5)
    for i in range(2):
        mid_x = solved(4 + i)
        for s in (2 * i, 2 * i + 1):
            scatter_start(2, part_c, recv_c, s, accum[s] + nn(mid_x, leaf_panels[s, 0]))
        share(i, 4 + i, mid_x)
    for s in range(4):
        lift(s)
    for i, slot in ((0, 2 * (1 - g)), (1, 2 * (1 - g) + 1), (2, 5 - g)):
        arrived(theirs.at[i], cross_send.at[n + i], cross_recv.at[n + i])
        store(theirs.at[i], upper_out_h.at[slot])
    for s in range(4):
        leaf_out[s] = solved(s)
        store(leaf_out.at[s], leaf_out_h.at[s])
    for copy in pending:
        copy.wait_send()
    for copy in stores:
        copy.wait()


def half_tree(
    n,
    leaf_rhs,
    upper_rhs,
    leaf_inv,
    upper_inv,
    leaf_panels,
    mid_panels,
    top_panels,
    leaf_widths,
    upper_widths,
):
    rows, width, count = leaf_inv.shape[1], leaf_inv.shape[2], leaf_rhs.shape[2]
    low = jnp.bfloat16
    hbm = pl.BlockSpec(memory_space=pltpu.HBM)
    leaf_t, upper_t = pl.pallas_call(
        functools.partial(tree_kernel, n),
        out_shape=[
            jax.ShapeDtypeStruct((4, count, rows), low),
            jax.ShapeDtypeStruct((7, count, rows), low),
        ],
        in_specs=[hbm] * 9,
        out_specs=[hbm, hbm],
        scratch_shapes=[
            pltpu.SMEM(leaf_widths.shape, jnp.int32),
            pltpu.SMEM(upper_widths.shape, jnp.int32),
            pltpu.VMEM((4, count, rows), low),
            pltpu.VMEM((7, count, rows), low),
            pltpu.VMEM((4, rows, width), low),
            pltpu.VMEM((4, rows, width), low),
            pltpu.VMEM((4, 3, rows, width), low),
            pltpu.VMEM((2, 2, rows, width), low),
            pltpu.VMEM((rows, width), low),
            pltpu.VMEM((7, count, width), low),
            pltpu.VMEM((7, count, width), low),
            pltpu.VMEM((2, count, width), low),
            pltpu.VMEM((7, count, width), low),
            pltpu.VMEM((8, count, width), low),
            pltpu.VMEM((7, n - 1, count, rows), low),
            pltpu.VMEM((8, n - 1, count, rows), low),
            pltpu.VMEM((6, count, width), jnp.float32),
            pltpu.VMEM((3, count, rows), low),
            pltpu.VMEM((3, count, rows), low),
            pltpu.VMEM((4, count, rows), low),
            pltpu.VMEM((count, rows), low),
            pltpu.SemaphoreType.DMA((19,)),
            pltpu.SemaphoreType.DMA((4, 8, n - 1)),
            pltpu.SemaphoreType.DMA((4, 8, n - 1)),
            pltpu.SemaphoreType.DMA((n + 3,)),
            pltpu.SemaphoreType.DMA((n + 3,)),
            pltpu.SemaphoreType.DMA((11,)),
        ],
        compiler_params=pltpu.CompilerParams(
            collective_id=0, has_side_effects=True, vmem_limit_bytes=58 * 1024 * 1024
        ),
    )(
        leaf_widths,
        upper_widths,
        jnp.swapaxes(leaf_rhs, 1, 2),
        jnp.swapaxes(upper_rhs, 1, 2),
        leaf_inv,
        upper_inv,
        leaf_panels,
        mid_panels,
        top_panels,
    )
    return jnp.swapaxes(leaf_t, 1, 2), jnp.swapaxes(upper_t, 1, 2)


def solution(mesh):
    in_specs = (
        P("subtree", "panel", "snap"),
        P(None, "panel", "snap"),
        P("subtree", "panel", None),
        P(None, "panel", None),
        P("subtree", None, "panel", None),
        P(None, None, "panel", None),
        P(None, "panel", None),
        P("subtree"),
        P(),
    )
    out_specs = (P("subtree", "panel", "snap"), P(None, "panel", "snap"))
    panel_count = mesh.shape["panel"]
    if mesh.shape["subtree"] == 2 and panel_count % 2 == 0:
        body = functools.partial(half_tree, panel_count)
    else:
        body = per_device
    return jax.shard_map(
        body, mesh=mesh, in_specs=in_specs, out_specs=out_specs, check_vma=False
    )
```

```python
import functools

import jax
import jax.numpy as jnp
from jax import lax
from jax.experimental import pallas as pl
from jax.experimental.pallas import tpu as pltpu
from jax.sharding import PartitionSpec as P


def live_mask(widths, full_width):
    return (jnp.arange(full_width, dtype=jnp.int32)[None, :] < widths[:, None]).astype(jnp.float32)


def own_rows(mask_full, own_count):
    return lax.dynamic_slice_in_dim(mask_full, lax.axis_index("panel") * own_count, own_count, 1)


def solve_down(inverse, reduced, mask_full):
    own_count = inverse.shape[1]
    live_cols = mask_full.astype(jnp.bfloat16)
    result = jnp.einsum(
        "nrw,nwc->nrc",
        inverse,
        lax.all_gather(reduced, "panel", axis=1, tiled=True) * live_cols[:, :, None],
        preferred_element_type=jnp.float32,
    )
    return (result * own_rows(mask_full, own_count)[:, :, None]).astype(jnp.bfloat16)


def spread(panels, solved):
    return jnp.einsum(
        "nkrw,nwc->nkrc",
        panels,
        lax.all_gather(solved, "panel", axis=1, tiled=True),
        preferred_element_type=jnp.float32,
    )


def ancestor_tables(global_index, level, count_up):
    offsets = [0, 0, 4, 6]
    slot_ids = jnp.arange(7, dtype=jnp.int32)
    tables = []
    for ancestor_rank in range(count_up):
        target = offsets[level + 1 + ancestor_rank] + jnp.right_shift(
            global_index, 1 + ancestor_rank
        )
        tables.append((slot_ids[None, :] == target[:, None]).astype(jnp.float32))
    return tables


def add_coupled(accum, coupled, tables):
    for ancestor_rank in range(len(tables)):
        accum = accum + jnp.einsum(
            "nrc,nu->urc",
            coupled[:, ancestor_rank],
            tables[ancestor_rank],
            precision=lax.Precision.HIGHEST,
        )
    return accum


def solve_up(inverse, panels, solved, upper_x, tables, mask_full):
    own_count = inverse.shape[1]
    if panels is None:
        reduced = solved
    else:
        picked = jnp.stack(
            [
                jnp.einsum(
                    "nu,urc->nrc",
                    table.astype(jnp.bfloat16),
                    upper_x,
                    preferred_element_type=jnp.float32,
                ).astype(jnp.bfloat16)
                for table in tables
            ],
            axis=1,
        )
        carried = lax.psum_scatter(
            jnp.einsum("nkrw,nkrc->wnc", panels, picked, preferred_element_type=jnp.float32).astype(
                jnp.bfloat16
            ),
            "panel",
            scatter_dimension=0,
            tiled=True,
        ).astype(jnp.float32)
        reduced = (solved.astype(jnp.float32) - jnp.transpose(carried, (1, 0, 2))).astype(
            jnp.bfloat16
        )
    own_live = own_rows(mask_full, own_count)
    masked = reduced * own_live[:, :, None].astype(jnp.bfloat16)
    summed = lax.psum_scatter(
        jnp.einsum("nrw,nrc->wnc", inverse, masked, preferred_element_type=jnp.float32).astype(
            jnp.bfloat16
        ),
        "panel",
        scatter_dimension=0,
        tiled=True,
    ).astype(jnp.float32)
    return (jnp.transpose(summed, (1, 0, 2)) * own_live[:, :, None]).astype(jnp.bfloat16)


def per_device(
    leaf_rhs,
    upper_rhs,
    leaf_inv,
    upper_inv,
    leaf_panels,
    mid_panels,
    top_panels,
    leaf_widths,
    upper_widths,
):
    full_width = leaf_inv.shape[2]
    own_count = leaf_inv.shape[1]
    leaf_count = leaf_inv.shape[0]
    groups = lax.axis_size("subtree")
    group_id = lax.axis_index("subtree")
    leaf_live = live_mask(leaf_widths, full_width)
    upper_live = live_mask(upper_widths, full_width)
    leaf_index = group_id * leaf_count + jnp.arange(leaf_count, dtype=jnp.int32)
    upper_index = jnp.arange(7, dtype=jnp.int32)
    leaf_tables = ancestor_tables(leaf_index, 0, 3)
    mid_tables = ancestor_tables(upper_index[0:4], 1, 2)
    high_tables = ancestor_tables(upper_index[4:6] - 4, 2, 1)
    top_stack = top_panels[:, None]
    leaf_sol = solve_down(leaf_inv, leaf_rhs, leaf_live)
    coupled_sum = jnp.zeros((7, own_count, leaf_rhs.shape[2]), jnp.float32)
    coupled_sum = add_coupled(coupled_sum, spread(leaf_panels, leaf_sol), leaf_tables)
    column_share = leaf_rhs.shape[2] // groups
    coupled_sum = lax.psum_scatter(
        coupled_sum.astype(jnp.bfloat16), "subtree", scatter_dimension=2, tiled=True
    ).astype(jnp.float32)
    upper_part = lax.dynamic_slice_in_dim(upper_rhs, group_id * column_share, column_share, 2)
    mid_sol = solve_down(
        upper_inv[0:4],
        (upper_part[0:4].astype(jnp.float32) - coupled_sum[0:4]).astype(jnp.bfloat16),
        upper_live[0:4],
    )
    coupled_sum = add_coupled(coupled_sum, spread(mid_panels, mid_sol), mid_tables)
    high_sol = solve_down(
        upper_inv[4:6],
        (upper_part[4:6].astype(jnp.float32) - coupled_sum[4:6]).astype(jnp.bfloat16),
        upper_live[4:6],
    )
    coupled_sum = add_coupled(coupled_sum, spread(top_stack, high_sol), high_tables)
    root_sol = solve_down(
        upper_inv[6:7],
        (upper_part[6:7].astype(jnp.float32) - coupled_sum[6:7]).astype(jnp.bfloat16),
        upper_live[6:7],
    )
    column_count = upper_part.shape[2]
    zero_mid = jnp.zeros((4, own_count, column_count), jnp.bfloat16)
    zero_high = jnp.zeros((2, own_count, column_count), jnp.bfloat16)
    root_x = solve_up(upper_inv[6:7], None, root_sol, None, None, upper_live[6:7])
    upper_x = jnp.concatenate([zero_mid, zero_high, root_x], axis=0)
    high_x = solve_up(upper_inv[4:6], top_stack, high_sol, upper_x, high_tables, upper_live[4:6])
    upper_x = jnp.concatenate([zero_mid, high_x, root_x], axis=0)
    mid_x = solve_up(upper_inv[0:4], mid_panels, mid_sol, upper_x, mid_tables, upper_live[0:4])
    upper_x = jnp.concatenate([mid_x, high_x, root_x], axis=0)
    upper_x = lax.all_gather(upper_x, "subtree", axis=2, tiled=True)
    leaf_x = solve_up(leaf_inv, leaf_panels, leaf_sol, upper_x, leaf_tables, leaf_live)
    return (leaf_x, upper_x)


def nt(left, right):
    return lax.dot_general(
        left, right, (((1,), (1,)), ((), ())), preferred_element_type=jnp.float32
    )


def nn(left, right):
    return jnp.dot(left, right, preferred_element_type=jnp.float32)


def tree_kernel(
    n,
    leaf_widths_h,
    upper_widths_h,
    leaf_rhs_h,
    upper_rhs_h,
    leaf_inv_h,
    upper_inv_h,
    leaf_panels_h,
    mid_panels_h,
    top_panels_h,
    leaf_out_h,
    upper_out_h,
    leaf_widths,
    upper_widths,
    leaf_rhs,
    upper_rhs,
    leaf_inv,
    upper_inv,
    leaf_panels,
    mid_panels,
    top_panel,
    r_full,
    y_full,
    root_full,
    part_c,
    part_s,
    recv_c,
    recv_s,
    accum,
    mine,
    theirs,
    leaf_out,
    sep_out,
    load_sem,
    send_sem,
    recv_sem,
    cross_send,
    cross_recv,
    store_sem,
):
    g = lax.axis_index("subtree")
    p = lax.axis_index("panel")
    rows = leaf_inv.shape[1]
    far = n // 2
    chip, core = p // 2, p % 2
    steps = list(range(2, n)) + [1]

    def ahead(k):
        return ((chip + k // 2) % far) * 2 + (core + k % 2) % 2

    def behind(k):
        return ((chip + far - k // 2) % far) * 2 + (core + k % 2) % 2

    def cols(index):
        return pl.ds(pl.multiple_of(index * rows, rows), rows)

    own = cols(p)

    barrier = pltpu.get_barrier_semaphore()
    for k in range(1, n):
        pl.semaphore_signal(barrier, inc=1, device_id={"panel": ahead(k)})
    for k in range(n):
        pl.semaphore_signal(barrier, inc=1, device_id={"subtree": 1 - g, "panel": ahead(k)})

    stores = []

    def store(src, dst):
        stores.append(pltpu.make_async_copy(src, dst, store_sem.at[len(stores)]))
        stores[-1].start()

    loads = {}

    def load(key, src, dst):
        loads[key] = pltpu.make_async_copy(src, dst, load_sem.at[len(loads)])
        loads[key].start()

    load("leaf_rhs", leaf_rhs_h, leaf_rhs)
    load("leaf_widths", leaf_widths_h, leaf_widths)
    load("upper_widths", upper_widths_h, upper_widths)
    for s in range(4):
        load(("inv", s), leaf_inv_h.at[s], leaf_inv.at[s])
    load("upper_rhs", upper_rhs_h, upper_rhs)
    for s in range(4):
        load(("pan", s), leaf_panels_h.at[s], leaf_panels.at[s])
    for i in range(2):
        load(("inv", 4 + i), upper_inv_h.at[2 * g + i], upper_inv.at[i])
    for i in range(2):
        load(("pan", 4 + i), mid_panels_h.at[2 * g + i], mid_panels.at[i])
    load(("inv", 6), upper_inv_h.at[4 + g], upper_inv.at[2])
    load(("pan", 6), top_panels_h.at[g], top_panel)
    load(("inv", 7), upper_inv_h.at[6], upper_inv.at[3])

    def inverse(s):
        return leaf_inv[s] if s < 4 else upper_inv[s - 4]

    upper_index = {4: 2 * g, 5: 2 * g + 1, 6: 4 + g, 7: 6}
    row_id = lax.broadcasted_iota(jnp.int32, (1, rows), 1) + p * rows

    def masked(s, value):
        width = leaf_widths[s] if s < 4 else upper_widths[upper_index[s]]
        return jnp.where(row_id < width, value, 0.0)

    pending = []

    def send(src, dst, ssem, rsem, device):
        copy = pltpu.make_async_remote_copy(
            src_ref=src, dst_ref=dst, send_sem=ssem, recv_sem=rsem, device_id=device
        )
        copy.start()
        pending.append(copy)

    def arrived(dst, ssem, rsem):
        pltpu.make_async_remote_copy(
            src_ref=dst, dst_ref=dst, send_sem=ssem, recv_sem=rsem, device_id={"panel": ahead(1)}
        ).wait_recv()

    def gather_start(e, full, s, value):
        full[s, :, own] = value
        for k in steps:
            block = full.at[s, :, own]
            send(block, block, send_sem.at[e, s, k - 1], recv_sem.at[e, s, k - 1], {"panel": ahead(k)})

    def gather_wait(e, full, s):
        for k in reversed(steps):
            arrived(full.at[s, :, cols(behind(k))], send_sem.at[e, s, k - 1], recv_sem.at[e, s, k - 1])
        return full[s]

    def scatter_start(e, part, recv, s, value):
        part[s] = value.astype(jnp.bfloat16)
        for k in steps:
            send(
                part.at[s, :, cols(ahead(k))],
                recv.at[s, k - 1],
                send_sem.at[e, s, k - 1],
                recv_sem.at[e, s, k - 1],
                {"panel": ahead(k)},
            )

    def scatter_wait(e, part, recv, s):
        total = part[s, :, own].astype(jnp.float32)
        for k in reversed(steps):
            arrived(recv.at[s, k - 1], send_sem.at[e, s, k - 1], recv_sem.at[e, s, k - 1])
            total = total + recv[s, k - 1].astype(jnp.float32)
        return total

    for key in ("leaf_rhs", "leaf_widths", "upper_widths"):
        loads[key].wait()
    rhs_masked = [masked(s, leaf_rhs[s].astype(jnp.float32)).astype(jnp.bfloat16) for s in range(4)]
    pl.semaphore_wait(barrier, 2 * n - 1)
    for s in range(4):
        gather_start(0, r_full, s, rhs_masked[s])

    def solve_y(s):
        full = gather_wait(0, r_full, s)
        loads[("inv", s)].wait()
        result = masked(s, nt(full, inverse(s))).astype(jnp.bfloat16)
        gather_start(1, y_full, s, result)

    def reduce_rhs(s, coupled):
        value = (upper_rhs[upper_index[s]].astype(jnp.float32) - coupled).astype(jnp.bfloat16)
        gather_start(0, r_full, s, masked(s, value.astype(jnp.float32)).astype(jnp.bfloat16))

    for s in range(4):
        solve_y(s)
    loads["upper_rhs"].wait()
    to_mid = []
    for s in range(4):
        full = gather_wait(1, y_full, s)
        loads[("pan", s)].wait()
        to_mid.append(nt(full, leaf_panels[s, 0]))
        if s % 2 == 1:
            reduce_rhs(4 + s // 2, to_mid[s - 1] + to_mid[s])
    to_high = nt(y_full[0], leaf_panels[0, 1])
    for s in range(1, 4):
        to_high = to_high + nt(y_full[s], leaf_panels[s, 1])
    solve_y(4)
    solve_y(5)
    to_root = nt(y_full[0], leaf_panels[0, 2])
    for s in range(1, 4):
        to_root = to_root + nt(y_full[s], leaf_panels[s, 2])
    for s in (4, 5):
        full = gather_wait(1, y_full, s)
        loads[("pan", s)].wait()
        to_high = to_high + nt(full, mid_panels[s - 4, 0])
    reduce_rhs(6, to_high)
    for s in (4, 5):
        to_root = to_root + nt(y_full[s], mid_panels[s - 4, 1])
    solve_y(6)
    full = gather_wait(1, y_full, 6)
    loads[("pan", 6)].wait()
    to_root = to_root + nt(full, top_panel[...])

    base = jnp.where(g == 0, upper_rhs[6].astype(jnp.float32), 0.0)
    root_full[g, :, own] = masked(7, base - to_root).astype(jnp.bfloat16)
    block = root_full.at[g, :, own]
    for k in steps + [0]:
        send(
            block,
            block,
            cross_send.at[k],
            cross_recv.at[k],
            {"subtree": 1 - g, "panel": ahead(k)},
        )
        if k > 0:
            send(block, block, send_sem.at[0, 7, k - 1], recv_sem.at[0, 7, k - 1], {"panel": ahead(k)})
    loads[("inv", 7)].wait()
    for k in reversed(steps):
        arrived(
            root_full.at[g, :, cols(behind(k))], send_sem.at[0, 7, k - 1], recv_sem.at[0, 7, k - 1]
        )
    for k in [0] + steps:
        arrived(root_full.at[1 - g, :, cols(behind(k))], cross_send.at[k], cross_recv.at[k])
    reduced = (root_full[0].astype(jnp.float32) + root_full[1].astype(jnp.float32)).astype(jnp.bfloat16)
    lifted = masked(7, nt(reduced, inverse(7))).astype(jnp.bfloat16)

    def lift(s):
        own_y = y_full[s, :, own].astype(jnp.float32)
        value = (own_y - scatter_wait(2, part_c, recv_c, s)).astype(jnp.bfloat16)
        value = masked(s, value.astype(jnp.float32)).astype(jnp.bfloat16)
        scatter_start(3, part_s, recv_s, s, nn(value, inverse(s)))

    def solved(s):
        return masked(s, scatter_wait(3, part_s, recv_s, s)).astype(jnp.bfloat16)

    scatter_start(3, part_s, recv_s, 7, nn(lifted, inverse(7)))
    root_x = solved(7)
    scatter_start(2, part_c, recv_c, 6, nn(root_x, top_panel[...]))
    sep_out[6] = root_x.astype(jnp.float32)
    store(sep_out.at[6], upper_out_h.at[6])
    for i in range(2):
        accum[4 + i] = nn(root_x, mid_panels[i, 1])
    lift(6)
    for s in range(4):
        accum[s] = nn(root_x, leaf_panels[s, 2])
    high_x = solved(6)
    for s in (4, 5):
        scatter_start(2, part_c, recv_c, s, accum[s] + nn(high_x, mid_panels[s - 4, 0]))

    def share(i, s, value):
        mine[i] = value
        sep_out[i] = value.astype(jnp.float32)
        store(sep_out.at[i], upper_out_h.at[upper_index[s]])
        send(mine.at[i], theirs.at[i], cross_send.at[n + i], cross_recv.at[n + i], {"subtree": 1 - g})

    share(2, 6, high_x)
    for s in range(4):
        accum[s] = accum[s] + nn(high_x, leaf_panels[s, 1])
    lift(4)
    lift(5)
    for i in range(2):
        mid_x = solved(4 + i)
        for s in (2 * i, 2 * i + 1):
            scatter_start(2, part_c, recv_c, s, accum[s] + nn(mid_x, leaf_panels[s, 0]))
        share(i, 4 + i, mid_x)
    for s in range(4):
        lift(s)
    for i, slot in ((0, 2 * (1 - g)), (1, 2 * (1 - g) + 1), (2, 5 - g)):
        arrived(theirs.at[i], cross_send.at[n + i], cross_recv.at[n + i])
        sep_out[3 + i] = theirs[i].astype(jnp.float32)
        store(sep_out.at[3 + i], upper_out_h.at[slot])
    for s in range(4):
        leaf_out[s] = masked(s, scatter_wait(3, part_s, recv_s, s))
        store(leaf_out.at[s], leaf_out_h.at[s])
    for copy in pending:
        copy.wait_send()
    for copy in stores:
        copy.wait()


def half_tree(
    n,
    leaf_rhs,
    upper_rhs,
    leaf_inv,
    upper_inv,
    leaf_panels,
    mid_panels,
    top_panels,
    leaf_widths,
    upper_widths,
):
    rows, width, count = leaf_inv.shape[1], leaf_inv.shape[2], leaf_rhs.shape[2]
    low = jnp.bfloat16
    hbm = pl.BlockSpec(memory_space=pltpu.HBM)
    leaf_t, upper_t = pl.pallas_call(
        functools.partial(tree_kernel, n),
        out_shape=[
            jax.ShapeDtypeStruct((4, count, rows), jnp.float32),
            jax.ShapeDtypeStruct((7, count, rows), jnp.float32),
        ],
        in_specs=[hbm] * 9,
        out_specs=[hbm, hbm],
        scratch_shapes=[
            pltpu.SMEM(leaf_widths.shape, jnp.int32),
            pltpu.SMEM(upper_widths.shape, jnp.int32),
            pltpu.VMEM((4, count, rows), low),
            pltpu.VMEM((7, count, rows), low),
            pltpu.VMEM((4, rows, width), low),
            pltpu.VMEM((4, rows, width), low),
            pltpu.VMEM((4, 3, rows, width), low),
            pltpu.VMEM((2, 2, rows, width), low),
            pltpu.VMEM((rows, width), low),
            pltpu.VMEM((7, count, width), low),
            pltpu.VMEM((7, count, width), low),
            pltpu.VMEM((2, count, width), low),
            pltpu.VMEM((7, count, width), low),
            pltpu.VMEM((8, count, width), low),
            pltpu.VMEM((7, n - 1, count, rows), low),
            pltpu.VMEM((8, n - 1, count, rows), low),
            pltpu.VMEM((6, count, width), jnp.float32),
            pltpu.VMEM((3, count, rows), low),
            pltpu.VMEM((3, count, rows), low),
            pltpu.VMEM((4, count, rows), jnp.float32),
            pltpu.VMEM((7, count, rows), jnp.float32),
            pltpu.SemaphoreType.DMA((19,)),
            pltpu.SemaphoreType.DMA((4, 8, n - 1)),
            pltpu.SemaphoreType.DMA((4, 8, n - 1)),
            pltpu.SemaphoreType.DMA((n + 3,)),
            pltpu.SemaphoreType.DMA((n + 3,)),
            pltpu.SemaphoreType.DMA((11,)),
        ],
        compiler_params=pltpu.CompilerParams(
            collective_id=0, has_side_effects=True, vmem_limit_bytes=58 * 1024 * 1024
        ),
    )(
        leaf_widths,
        upper_widths,
        jnp.swapaxes(leaf_rhs, 1, 2),
        jnp.swapaxes(upper_rhs, 1, 2),
        leaf_inv,
        upper_inv,
        leaf_panels,
        mid_panels,
        top_panels,
    )
    return jnp.swapaxes(leaf_t.astype(low), 1, 2), jnp.swapaxes(upper_t.astype(low), 1, 2)


def solution(mesh):
    in_specs = (
        P("subtree", "panel", "snap"),
        P(None, "panel", "snap"),
        P("subtree", "panel", None),
        P(None, "panel", None),
        P("subtree", None, "panel", None),
        P(None, None, "panel", None),
        P(None, "panel", None),
        P("subtree"),
        P(),
    )
    out_specs = (P("subtree", "panel", "snap"), P(None, "panel", "snap"))
    panel_count = mesh.shape["panel"]
    if mesh.shape["subtree"] == 2 and panel_count % 2 == 0:
        body = functools.partial(half_tree, panel_count)
    else:
        body = per_device
    return jax.shard_map(
        body, mesh=mesh, in_specs=in_specs, out_specs=out_specs, check_vma=False
    )
```

```python
import functools

import jax
import jax.numpy as jnp
from jax import lax
from jax.experimental import pallas as pl
from jax.experimental.pallas import tpu as pltpu
from jax.sharding import PartitionSpec as P


def live_mask(widths, full_width):
    return (jnp.arange(full_width, dtype=jnp.int32)[None, :] < widths[:, None]).astype(jnp.float32)


def own_rows(mask_full, own_count):
    return lax.dynamic_slice_in_dim(mask_full, lax.axis_index("panel") * own_count, own_count, 1)


def solve_down(inverse, reduced, mask_full):
    own_count = inverse.shape[1]
    live_cols = mask_full.astype(jnp.bfloat16)
    result = jnp.einsum(
        "nrw,nwc->nrc",
        inverse,
        lax.all_gather(reduced, "panel", axis=1, tiled=True) * live_cols[:, :, None],
        preferred_element_type=jnp.float32,
    )
    return (result * own_rows(mask_full, own_count)[:, :, None]).astype(jnp.bfloat16)


def spread(panels, solved):
    return jnp.einsum(
        "nkrw,nwc->nkrc",
        panels,
        lax.all_gather(solved, "panel", axis=1, tiled=True),
        preferred_element_type=jnp.float32,
    )


def ancestor_tables(global_index, level, count_up):
    offsets = [0, 0, 4, 6]
    slot_ids = jnp.arange(7, dtype=jnp.int32)
    tables = []
    for ancestor_rank in range(count_up):
        target = offsets[level + 1 + ancestor_rank] + jnp.right_shift(
            global_index, 1 + ancestor_rank
        )
        tables.append((slot_ids[None, :] == target[:, None]).astype(jnp.float32))
    return tables


def add_coupled(accum, coupled, tables):
    for ancestor_rank in range(len(tables)):
        accum = accum + jnp.einsum(
            "nrc,nu->urc",
            coupled[:, ancestor_rank],
            tables[ancestor_rank],
            precision=lax.Precision.HIGHEST,
        )
    return accum


def solve_up(inverse, panels, solved, upper_x, tables, mask_full):
    own_count = inverse.shape[1]
    if panels is None:
        reduced = solved
    else:
        picked = jnp.stack(
            [
                jnp.einsum(
                    "nu,urc->nrc",
                    table.astype(jnp.bfloat16),
                    upper_x,
                    preferred_element_type=jnp.float32,
                ).astype(jnp.bfloat16)
                for table in tables
            ],
            axis=1,
        )
        carried = lax.psum_scatter(
            jnp.einsum("nkrw,nkrc->wnc", panels, picked, preferred_element_type=jnp.float32).astype(
                jnp.bfloat16
            ),
            "panel",
            scatter_dimension=0,
            tiled=True,
        ).astype(jnp.float32)
        reduced = (solved.astype(jnp.float32) - jnp.transpose(carried, (1, 0, 2))).astype(
            jnp.bfloat16
        )
    own_live = own_rows(mask_full, own_count)
    masked = reduced * own_live[:, :, None].astype(jnp.bfloat16)
    summed = lax.psum_scatter(
        jnp.einsum("nrw,nrc->wnc", inverse, masked, preferred_element_type=jnp.float32).astype(
            jnp.bfloat16
        ),
        "panel",
        scatter_dimension=0,
        tiled=True,
    ).astype(jnp.float32)
    return (jnp.transpose(summed, (1, 0, 2)) * own_live[:, :, None]).astype(jnp.bfloat16)


def per_device(
    leaf_rhs,
    upper_rhs,
    leaf_inv,
    upper_inv,
    leaf_panels,
    mid_panels,
    top_panels,
    leaf_widths,
    upper_widths,
):
    full_width = leaf_inv.shape[2]
    own_count = leaf_inv.shape[1]
    leaf_count = leaf_inv.shape[0]
    groups = lax.axis_size("subtree")
    group_id = lax.axis_index("subtree")
    leaf_live = live_mask(leaf_widths, full_width)
    upper_live = live_mask(upper_widths, full_width)
    leaf_index = group_id * leaf_count + jnp.arange(leaf_count, dtype=jnp.int32)
    upper_index = jnp.arange(7, dtype=jnp.int32)
    leaf_tables = ancestor_tables(leaf_index, 0, 3)
    mid_tables = ancestor_tables(upper_index[0:4], 1, 2)
    high_tables = ancestor_tables(upper_index[4:6] - 4, 2, 1)
    top_stack = top_panels[:, None]
    leaf_sol = solve_down(leaf_inv, leaf_rhs, leaf_live)
    coupled_sum = jnp.zeros((7, own_count, leaf_rhs.shape[2]), jnp.float32)
    coupled_sum = add_coupled(coupled_sum, spread(leaf_panels, leaf_sol), leaf_tables)
    column_share = leaf_rhs.shape[2] // groups
    coupled_sum = lax.psum_scatter(
        coupled_sum.astype(jnp.bfloat16), "subtree", scatter_dimension=2, tiled=True
    ).astype(jnp.float32)
    upper_part = lax.dynamic_slice_in_dim(upper_rhs, group_id * column_share, column_share, 2)
    mid_sol = solve_down(
        upper_inv[0:4],
        (upper_part[0:4].astype(jnp.float32) - coupled_sum[0:4]).astype(jnp.bfloat16),
        upper_live[0:4],
    )
    coupled_sum = add_coupled(coupled_sum, spread(mid_panels, mid_sol), mid_tables)
    high_sol = solve_down(
        upper_inv[4:6],
        (upper_part[4:6].astype(jnp.float32) - coupled_sum[4:6]).astype(jnp.bfloat16),
        upper_live[4:6],
    )
    coupled_sum = add_coupled(coupled_sum, spread(top_stack, high_sol), high_tables)
    root_sol = solve_down(
        upper_inv[6:7],
        (upper_part[6:7].astype(jnp.float32) - coupled_sum[6:7]).astype(jnp.bfloat16),
        upper_live[6:7],
    )
    column_count = upper_part.shape[2]
    zero_mid = jnp.zeros((4, own_count, column_count), jnp.bfloat16)
    zero_high = jnp.zeros((2, own_count, column_count), jnp.bfloat16)
    root_x = solve_up(upper_inv[6:7], None, root_sol, None, None, upper_live[6:7])
    upper_x = jnp.concatenate([zero_mid, zero_high, root_x], axis=0)
    high_x = solve_up(upper_inv[4:6], top_stack, high_sol, upper_x, high_tables, upper_live[4:6])
    upper_x = jnp.concatenate([zero_mid, high_x, root_x], axis=0)
    mid_x = solve_up(upper_inv[0:4], mid_panels, mid_sol, upper_x, mid_tables, upper_live[0:4])
    upper_x = jnp.concatenate([mid_x, high_x, root_x], axis=0)
    upper_x = lax.all_gather(upper_x, "subtree", axis=2, tiled=True)
    leaf_x = solve_up(leaf_inv, leaf_panels, leaf_sol, upper_x, leaf_tables, leaf_live)
    return (leaf_x, upper_x)


def nt(left, right):
    return lax.dot_general(
        left, right, (((1,), (1,)), ((), ())), preferred_element_type=jnp.float32
    )


def nn(left, right):
    return jnp.dot(left, right, preferred_element_type=jnp.float32)


def tree_kernel(
    n,
    leaf_widths_h,
    upper_widths_h,
    leaf_rhs_h,
    upper_rhs_h,
    leaf_inv_h,
    upper_inv_h,
    leaf_panels_h,
    mid_panels_h,
    top_panels_h,
    leaf_out,
    upper_out,
    leaf_widths,
    upper_widths,
    leaf_rhs,
    upper_rhs,
    leaf_inv,
    upper_inv,
    leaf_panels,
    mid_panels,
    top_panel,
    r_full,
    y_full,
    root_full,
    part_c,
    part_s,
    recv_c,
    recv_s,
    accum,
    mine,
    theirs,
    load_sem,
    send_sem,
    recv_sem,
    cross_send,
    cross_recv,
):
    g = lax.axis_index("subtree")
    p = lax.axis_index("panel")
    rows = leaf_inv.shape[1]
    far = n // 2
    chip, core = p // 2, p % 2
    steps = list(range(2, n)) + [1]

    def ahead(k):
        return ((chip + k // 2) % far) * 2 + (core + k % 2) % 2

    def behind(k):
        return ((chip + far - k // 2) % far) * 2 + (core + k % 2) % 2

    def cols(index):
        return pl.ds(pl.multiple_of(index * rows, rows), rows)

    own = cols(p)

    barrier = pltpu.get_barrier_semaphore()
    for k in range(1, n):
        pl.semaphore_signal(barrier, inc=1, device_id={"panel": ahead(k)})
    for k in range(n):
        pl.semaphore_signal(barrier, inc=1, device_id={"subtree": 1 - g, "panel": ahead(k)})

    loads = {}

    def load(key, src, dst):
        loads[key] = pltpu.make_async_copy(src, dst, load_sem.at[len(loads)])
        loads[key].start()

    load("leaf_rhs", leaf_rhs_h, leaf_rhs)
    load("leaf_widths", leaf_widths_h, leaf_widths)
    load("upper_widths", upper_widths_h, upper_widths)
    for s in range(4):
        load(("inv", s), leaf_inv_h.at[s], leaf_inv.at[s])
    load("upper_rhs", upper_rhs_h, upper_rhs)
    for s in range(4):
        load(("pan", s), leaf_panels_h.at[s], leaf_panels.at[s])
    for i in range(2):
        load(("inv", 4 + i), upper_inv_h.at[2 * g + i], upper_inv.at[i])
    for i in range(2):
        load(("pan", 4 + i), mid_panels_h.at[2 * g + i], mid_panels.at[i])
    load(("inv", 6), upper_inv_h.at[4 + g], upper_inv.at[2])
    load(("pan", 6), top_panels_h.at[g], top_panel)
    load(("inv", 7), upper_inv_h.at[6], upper_inv.at[3])

    def inverse(s):
        return leaf_inv[s] if s < 4 else upper_inv[s - 4]

    upper_index = {4: 2 * g, 5: 2 * g + 1, 6: 4 + g, 7: 6}
    row_id = lax.broadcasted_iota(jnp.int32, (1, rows), 1) + p * rows

    def masked(s, value):
        width = leaf_widths[s] if s < 4 else upper_widths[upper_index[s]]
        return jnp.where(row_id < width, value, 0.0)

    pending = []

    def send(src, dst, ssem, rsem, device):
        copy = pltpu.make_async_remote_copy(
            src_ref=src, dst_ref=dst, send_sem=ssem, recv_sem=rsem, device_id=device
        )
        copy.start()
        pending.append(copy)

    def arrived(dst, ssem, rsem):
        pltpu.make_async_remote_copy(
            src_ref=dst, dst_ref=dst, send_sem=ssem, recv_sem=rsem, device_id={"panel": ahead(1)}
        ).wait_recv()

    def gather_start(e, full, s, value):
        full[s, :, own] = value
        for k in steps:
            block = full.at[s, :, own]
            send(block, block, send_sem.at[e, s, k - 1], recv_sem.at[e, s, k - 1], {"panel": ahead(k)})

    def gather_wait(e, full, s):
        for k in reversed(steps):
            arrived(full.at[s, :, cols(behind(k))], send_sem.at[e, s, k - 1], recv_sem.at[e, s, k - 1])
        return full[s]

    def scatter_start(e, part, recv, s, value):
        part[s] = value.astype(jnp.bfloat16)
        for k in steps:
            send(
                part.at[s, :, cols(ahead(k))],
                recv.at[s, k - 1],
                send_sem.at[e, s, k - 1],
                recv_sem.at[e, s, k - 1],
                {"panel": ahead(k)},
            )

    def scatter_wait(e, part, recv, s):
        total = part[s, :, own].astype(jnp.float32)
        for k in reversed(steps):
            arrived(recv.at[s, k - 1], send_sem.at[e, s, k - 1], recv_sem.at[e, s, k - 1])
            total = total + recv[s, k - 1].astype(jnp.float32)
        return total

    for key in ("leaf_rhs", "leaf_widths", "upper_widths"):
        loads[key].wait()
    rhs_masked = [masked(s, leaf_rhs[s].astype(jnp.float32)).astype(jnp.bfloat16) for s in range(4)]
    pl.semaphore_wait(barrier, 2 * n - 1)
    for s in range(4):
        gather_start(0, r_full, s, rhs_masked[s])

    def solve_y(s):
        full = gather_wait(0, r_full, s)
        loads[("inv", s)].wait()
        result = masked(s, nt(full, inverse(s))).astype(jnp.bfloat16)
        gather_start(1, y_full, s, result)

    def reduce_rhs(s, coupled):
        value = (upper_rhs[upper_index[s]].astype(jnp.float32) - coupled).astype(jnp.bfloat16)
        gather_start(0, r_full, s, masked(s, value.astype(jnp.float32)).astype(jnp.bfloat16))

    for s in range(4):
        solve_y(s)
    loads["upper_rhs"].wait()
    to_mid = []
    for s in range(4):
        full = gather_wait(1, y_full, s)
        loads[("pan", s)].wait()
        to_mid.append(nt(full, leaf_panels[s, 0]))
        if s % 2 == 1:
            reduce_rhs(4 + s // 2, to_mid[s - 1] + to_mid[s])
    to_high = nt(y_full[0], leaf_panels[0, 1])
    for s in range(1, 4):
        to_high = to_high + nt(y_full[s], leaf_panels[s, 1])
    solve_y(4)
    solve_y(5)
    to_root = nt(y_full[0], leaf_panels[0, 2])
    for s in range(1, 4):
        to_root = to_root + nt(y_full[s], leaf_panels[s, 2])
    for s in (4, 5):
        full = gather_wait(1, y_full, s)
        loads[("pan", s)].wait()
        to_high = to_high + nt(full, mid_panels[s - 4, 0])
    reduce_rhs(6, to_high)
    for s in (4, 5):
        to_root = to_root + nt(y_full[s], mid_panels[s - 4, 1])
    solve_y(6)
    full = gather_wait(1, y_full, 6)
    loads[("pan", 6)].wait()
    to_root = to_root + nt(full, top_panel[...])

    base = jnp.where(g == 0, upper_rhs[6].astype(jnp.float32), 0.0)
    root_full[g, :, own] = masked(7, base - to_root).astype(jnp.bfloat16)
    block = root_full.at[g, :, own]
    for k in steps + [0]:
        send(
            block,
            block,
            cross_send.at[k],
            cross_recv.at[k],
            {"subtree": 1 - g, "panel": ahead(k)},
        )
        if k > 0:
            send(block, block, send_sem.at[0, 7, k - 1], recv_sem.at[0, 7, k - 1], {"panel": ahead(k)})
    loads[("inv", 7)].wait()
    for k in reversed(steps):
        arrived(
            root_full.at[g, :, cols(behind(k))], send_sem.at[0, 7, k - 1], recv_sem.at[0, 7, k - 1]
        )
    for k in [0] + steps:
        arrived(root_full.at[1 - g, :, cols(behind(k))], cross_send.at[k], cross_recv.at[k])
    reduced = (root_full[0].astype(jnp.float32) + root_full[1].astype(jnp.float32)).astype(jnp.bfloat16)
    lifted = masked(7, nt(reduced, inverse(7))).astype(jnp.bfloat16)

    def lift(s):
        own_y = y_full[s, :, own].astype(jnp.float32)
        value = (own_y - scatter_wait(2, part_c, recv_c, s)).astype(jnp.bfloat16)
        value = masked(s, value.astype(jnp.float32)).astype(jnp.bfloat16)
        scatter_start(3, part_s, recv_s, s, nn(value, inverse(s)))

    def solved(s):
        return masked(s, scatter_wait(3, part_s, recv_s, s)).astype(jnp.bfloat16)

    scatter_start(3, part_s, recv_s, 7, nn(lifted, inverse(7)))
    root_x = solved(7)
    scatter_start(2, part_c, recv_c, 6, nn(root_x, top_panel[...]))
    upper_out[6] = root_x
    for i in range(2):
        accum[4 + i] = nn(root_x, mid_panels[i, 1])
    lift(6)
    for s in range(4):
        accum[s] = nn(root_x, leaf_panels[s, 2])
    high_x = solved(6)
    for s in (4, 5):
        scatter_start(2, part_c, recv_c, s, accum[s] + nn(high_x, mid_panels[s - 4, 0]))

    def share(i, s, value):
        upper_out[upper_index[s]] = value
        mine[i] = value
        send(mine.at[i], theirs.at[i], cross_send.at[n + i], cross_recv.at[n + i], {"subtree": 1 - g})

    share(2, 6, high_x)
    for s in range(4):
        accum[s] = accum[s] + nn(high_x, leaf_panels[s, 1])
    lift(4)
    lift(5)
    for i in range(2):
        mid_x = solved(4 + i)
        for s in (2 * i, 2 * i + 1):
            scatter_start(2, part_c, recv_c, s, accum[s] + nn(mid_x, leaf_panels[s, 0]))
        share(i, 4 + i, mid_x)
    for s in range(4):
        lift(s)
    for i, slot in ((0, 2 * (1 - g)), (1, 2 * (1 - g) + 1), (2, 5 - g)):
        arrived(theirs.at[i], cross_send.at[n + i], cross_recv.at[n + i])
        upper_out[slot] = theirs[i]
    for s in range(4):
        leaf_out[s] = solved(s)
    for copy in pending:
        copy.wait_send()


def half_tree(
    n,
    leaf_rhs,
    upper_rhs,
    leaf_inv,
    upper_inv,
    leaf_panels,
    mid_panels,
    top_panels,
    leaf_widths,
    upper_widths,
):
    rows, width, count = leaf_inv.shape[1], leaf_inv.shape[2], leaf_rhs.shape[2]
    low = jnp.bfloat16
    vmem = pl.BlockSpec(memory_space=pltpu.VMEM)
    hbm = pl.BlockSpec(memory_space=pltpu.HBM)
    leaf_t, upper_t = pl.pallas_call(
        functools.partial(tree_kernel, n),
        out_shape=[
            jax.ShapeDtypeStruct((4, count, rows), low),
            jax.ShapeDtypeStruct((7, count, rows), low),
        ],
        in_specs=[hbm] * 9,
        out_specs=[vmem, vmem],
        scratch_shapes=[
            pltpu.SMEM(leaf_widths.shape, jnp.int32),
            pltpu.SMEM(upper_widths.shape, jnp.int32),
            pltpu.VMEM((4, count, rows), low),
            pltpu.VMEM((7, count, rows), low),
            pltpu.VMEM((4, rows, width), low),
            pltpu.VMEM((4, rows, width), low),
            pltpu.VMEM((4, 3, rows, width), low),
            pltpu.VMEM((2, 2, rows, width), low),
            pltpu.VMEM((rows, width), low),
            pltpu.VMEM((7, count, width), low),
            pltpu.VMEM((7, count, width), low),
            pltpu.VMEM((2, count, width), low),
            pltpu.VMEM((7, count, width), low),
            pltpu.VMEM((8, count, width), low),
            pltpu.VMEM((7, n - 1, count, rows), low),
            pltpu.VMEM((8, n - 1, count, rows), low),
            pltpu.VMEM((6, count, width), jnp.float32),
            pltpu.VMEM((3, count, rows), low),
            pltpu.VMEM((3, count, rows), low),
            pltpu.SemaphoreType.DMA((19,)),
            pltpu.SemaphoreType.DMA((4, 8, n - 1)),
            pltpu.SemaphoreType.DMA((4, 8, n - 1)),
            pltpu.SemaphoreType.DMA((n + 3,)),
            pltpu.SemaphoreType.DMA((n + 3,)),
        ],
        compiler_params=pltpu.CompilerParams(
            collective_id=0, has_side_effects=True, vmem_limit_bytes=(53 * 1024 + 736) * 1024
        ),
    )(
        leaf_widths,
        upper_widths,
        jnp.swapaxes(leaf_rhs, 1, 2),
        jnp.swapaxes(upper_rhs, 1, 2),
        leaf_inv,
        upper_inv,
        leaf_panels,
        mid_panels,
        top_panels,
    )
    return jnp.swapaxes(leaf_t, 1, 2), jnp.swapaxes(upper_t, 1, 2)


def solution(mesh):
    in_specs = (
        P("subtree", "panel", "snap"),
        P(None, "panel", "snap"),
        P("subtree", "panel", None),
        P(None, "panel", None),
        P("subtree", None, "panel", None),
        P(None, None, "panel", None),
        P(None, "panel", None),
        P("subtree"),
        P(),
    )
    out_specs = (P("subtree", "panel", "snap"), P(None, "panel", "snap"))
    panel_count = mesh.shape["panel"]
    if mesh.shape["subtree"] == 2 and panel_count % 2 == 0:
        body = functools.partial(half_tree, panel_count)
    else:
        body = per_device
    return jax.shard_map(
        body, mesh=mesh, in_specs=in_specs, out_specs=out_specs, check_vma=False
    )
```
